32 devices in a mesh: row: 8 (over z, x), col: 4 (over y, core).
Axes of the slice: x: 2, y: 2, z: 4, core: 2. Of those that a mesh axis runs over, the one named last changes fastest.
Arguments:
- points: float32 [4096, 256], P('row'), may hold values from -6 to 6
- nugget: float32 [4096], P('row'), may hold values from 0.5 to 2
- weights: float32 [256], replicated, may hold values from 0.0005 to 0.005
- band_start: int32 [8], replicated, may hold values from 0 to 6, as said below
Outputs:
- factored: float32 [8, 2, 4, 512, 512], P('row', None, 'col')
The draws below stay inside these ranges and needn't reach their ends.
Inputs may be any that keep to these rules, and one draw needn't show every extreme that they name: band_start[i] <= i - 1 for every i >= 1, band_start[0] = 0; band_start[5] = 0; the last tile row has band_start = 6.
All inputs are finite; a program needn't handle non-finite values.
Results may differ from the reference program's by a relative error of at most 0.0003.
Values sent between devices are 32-bit elements; how exact they have to be, the bound alone decides.
A program may use at most 128 MiB of HBM per device.

```python
import math
import jax
import jax.numpy as jnp
from jax import lax

TILE = 512
COV = 256
NT = 8
KC = 2
NPTS = 4096
N_COL = 4


def draw_band_start(key, part):
    rows = jnp.arange(NT, dtype=jnp.int32)
    reach = jax.random.randint(key, (NT,), 1, NT // 2 + 1).astype(jnp.int32)
    reach = reach.at[NT // 2 + 1].set(NT)
    reach = reach.at[NT - 1].set(1)
    return jnp.maximum(rows - reach, 0).astype(jnp.int32)


def levels(rng, shape, pieces, low, largest):
    gain = 1.0
    for axis_at, parts in pieces:
        draws = jax.random.uniform(jax.random.fold_in(jax.random.fold_in(rng, 6), axis_at), (parts,), jnp.float32, low / len(pieces), largest / len(pieces))
        gain = gain * jnp.repeat(jnp.exp(draws), shape[axis_at] // parts).reshape((-1,) + (1,) * (len(shape) - 1 - axis_at))
    return gain


def bell_draw(rng, dims, deviation, most, shards=(), kind=jnp.bfloat16):
    array = deviation * jax.random.normal(rng, dims, jnp.float32)
    if shards:
        array = array * levels(rng, dims, shards, -0.22, 0.18)
    return jnp.clip(array, -most, most).astype(kind)


def setup_inputs(seed: int = 0) -> dict:
    seeds = jax.random.split(jax.random.key(seed), 5)
    points = bell_draw(seeds[0], (NPTS, COV), 1.0, 6.0, ((0, 8),), jnp.float32)
    nugget = jnp.clip(jnp.exp(math.log(2.0) - 1.3862944 * jax.random.uniform(seeds[1], (NPTS,), jnp.float32) ** levels(seeds[1], (NPTS,), ((0, 8),), -0.2, 0.2)), 0.5, 2.0)
    weights = jnp.clip(jnp.exp(jax.random.uniform(seeds[2], (COV,), jnp.float32, math.log(0.0005), math.log(0.005))), 0.0005, 0.005)
    band_start = draw_band_start(jax.random.fold_in(seeds[4], 71), 0)
    return {"points": points, "nugget": nugget, "weights": weights, "band_start": band_start}


def kernel_tile(xrow, xcol, weights):
    weighted = xrow * weights
    sq_row = lax.optimization_barrier(jnp.sum(weighted * xrow, axis=1))
    sq_col = lax.optimization_barrier(jnp.sum(xcol * xcol * weights, axis=1))
    cross = jnp.dot(weighted.astype(jnp.float32), xcol.T.astype(jnp.float32), precision=lax.Precision.HIGHEST, preferred_element_type=jnp.float32)
    dist_sq = jnp.maximum(sq_row[:, None] + sq_col[None, :] - 2.0 * cross, 0.0)
    dist = jnp.sqrt(3.0 * dist_sq)
    return (1.0 + dist) * jnp.exp(-dist)

def reference(points, nugget, weights, band_start):
    tiles_x = points.reshape(NT, TILE, COV)
    tiles_n = nugget.reshape(NT, TILE)
    indices = jnp.arange(NT, dtype=jnp.int32)

    def build_row(i):

        def build(j):
            block = kernel_tile(tiles_x[i], tiles_x[j], weights)
            keep = (j >= band_start[i]) & (j <= i)
            block = jnp.where(keep, block, jnp.float32(0.0))
            return block + jnp.where(j == i, jnp.diag(tiles_n[i]), jnp.float32(0.0))
        return lax.map(build, indices)
    matrix = lax.map(build_row, indices)
    for p in range(2):
        lpp = jnp.linalg.cholesky(matrix[p, p])
        solved = jax.vmap(lambda blk: jax.scipy.linalg.solve_triangular(lpp, blk.T, lower=True).T)(matrix[:, p])
        panel = jnp.where((indices > p)[:, None, None], solved, jnp.float32(0.0))
        panel = jnp.where((indices == p)[:, None, None], lpp[None], panel)

        def update(i):
            rowtiles = matrix[i]
            prod = jnp.einsum('ab,jcb->jac', panel[i], panel, precision=lax.Precision.HIGHEST)
            live = (indices > p) & (indices <= i)
            rowtiles = rowtiles - jnp.where(live[:, None, None], prod, jnp.float32(0.0))
            return jnp.where((indices == p)[:, None, None], panel[i][None], rowtiles)
        matrix = lax.map(update, indices)
    return matrix.reshape(NT, KC, N_COL, TILE, TILE)
```

```python
import functools

import jax
import jax.numpy as jnp
from jax import lax
from jax.experimental import pallas as pl
from jax.experimental.pallas import tpu as pltpu
from jax.sharding import PartitionSpec as P

F32 = jnp.float32
BF16 = jnp.bfloat16
NB = 128
GROUP = 4
NT_DIMS = (((1,), (1,)), ((), ()))
TN_DIMS = (((0,), (0,)), ((), ()))
NN_DIMS = (((1,), (0,)), ((), ()))


def split(x):
    hi = x.astype(BF16)
    return hi, (x - hi.astype(F32)).astype(BF16)


def dot3(a, b, dims):
    def one(x, y):
        return lax.dot_general(x, y, dims, preferred_element_type=F32)

    return one(a[0], b[0]) + (one(a[0], b[1]) + one(a[1], b[0]))


def wide(x):
    return jnp.broadcast_to(x, (8, NB))


def invert_factor(aug, w_ref, k):
    n_slab = NB // 8
    at = pl.multiple_of(k * NB, NB)
    block = aug[pl.ds(at, NB), pl.ds(at, NB)]
    lane = lax.broadcasted_iota(jnp.int32, (8, NB), 1)
    sub = lax.broadcasted_iota(jnp.int32, (8, NB), 0)
    s = [block[8 * t : 8 * t + 8, :] for t in range(n_slab)]
    v = [jnp.where(lane == sub + 8 * t, 1.0, 0.0).astype(F32) for t in range(n_slab)]
    for j in range(0, NB, GROUP):
        first = j // 8
        rows = [wide(s[first][j % 8 + g : j % 8 + g + 1, :]) for g in range(GROUP)]
        vrows = [wide(v[first][j % 8 + g : j % 8 + g + 1, :]) for g in range(GROUP)]
        last = (j + GROUP) // 8
        cols = [
            {t: wide(s[t][:, j + g : j + g + 1]) for t in range(last, n_slab)}
            for g in range(GROUP)
        ]
        piv = [
            {h: wide(rows[g][:, j + h : j + h + 1]) for h in range(g, GROUP)}
            for g in range(GROUP)
        ]
        for g in range(GROUP):
            root = lax.rsqrt(piv[g][g])
            inv = root * root
            w_ref[j + g : j + g + 1, :] = (vrows[g] * root)[0:1, :]
            for h in range(g + 1, GROUP):
                f = piv[g][h] * inv
                for m in range(h, GROUP):
                    piv[h][m] = piv[h][m] - f * piv[g][m]
                rows[h] = rows[h] - f * rows[g]
                vrows[h] = vrows[h] - f * vrows[g]
                for t in cols[h]:
                    cols[h][t] = cols[h][t] - f * cols[g][t]
            q = rows[g] * inv
            vq = vrows[g] * inv
            for t in cols[g]:
                s[t] = s[t] - cols[g][t] * q
                v[t] = v[t] - cols[g][t] * vq


def factor(aug, u_ref, wh, wl, wk):
    size = aug.shape[0]
    n_block = size // NB
    row = lax.broadcasted_iota(jnp.int32, (size, size), 0)
    col = lax.broadcasted_iota(jnp.int32, (size, size), 1)
    aug[:, size:] = jnp.where(row == col, 1.0, 0.0).astype(F32)

    @pl.loop(0, n_block)
    def _(k):
        invert_factor(aug, wk, k)
        winv = split(wk[...])
        for kk in range(n_block):

            @pl.when(k == kk)
            def _():
                lo, hi = kk * NB, size + (kk + 1) * NB
                strip = dot3(winv, split(aug[lo : lo + NB, lo:hi]), NN_DIMS)
                parts = split(strip)
                u_ref[lo : lo + NB, lo:] = strip[:, : size - lo]
                wh[lo : lo + NB, : lo + NB] = parts[0][:, size - lo :]
                wl[lo : lo + NB, : lo + NB] = parts[1][:, size - lo :]
                if lo + NB < size:
                    zero = jnp.zeros((NB, size - lo - NB), BF16)
                    wh[lo : lo + NB, lo + NB :] = zero
                    wl[lo : lo + NB, lo + NB :] = zero
                    left = tuple(x[:, NB : size - lo] for x in parts)
                    right = tuple(x[:, NB:] for x in parts)
                    aug[lo + NB :, lo + NB : hi] -= dot3(left, right, TN_DIMS)


def prepare(y, slot, yh, yl, scol, srow):
    hi, lo = split(y)
    yh[slot], yl[slot] = hi, lo
    sq = y * y
    scol[slot] = jnp.sum(sq, axis=1, keepdims=True)
    srow[slot] = lax.dot_general(
        jnp.ones((8, y.shape[1]), F32), sq, NT_DIMS,
        precision=lax.Precision.HIGHEST, preferred_element_type=F32,
    )


def compute(i, c, n_col, blocks, g_ref, root_ref, band_ref, out_ref,
            aug, u_ref, wh, wl, wk, p0h, p0l, p1h, p1l, yh, yl, scol, srow):
    size = aug.shape[0]
    cov = g_ref.shape[-1]
    tiles = [0, 1, i] + [c + n_col * k for k in range(blocks)]

    def kernel_at(a, b, ta, tb, nugget=False):
        cross = dot3((yh[a], yl[a]), (yh[b], yl[b]), NT_DIMS)
        dist_sq = jnp.maximum(scol[a] + srow[b][0:1, :] - 2.0 * cross, 0.0)
        dist = jnp.sqrt(3.0 * dist_sq)
        value = (1.0 + dist) * jnp.exp(-dist)
        keep = (tb >= band_ref[ta]) & (tb <= ta)
        value = jnp.where(keep, value, 0.0)
        if nugget:
            extra = jnp.concatenate(
                [g_ref[ta, size + r : size + r + 1, :] for r in range(size // cov)], axis=1
            )
            row = lax.broadcasted_iota(jnp.int32, (size, size), 0)
            col = lax.broadcasted_iota(jnp.int32, (size, size), 1)
            value = value + jnp.where((row == col) & (ta == tb), extra, 0.0)
        return value

    for slot, t in enumerate(tiles):
        y = g_ref[t, :size, :] * root_ref[...]
        prepare(y, slot, yh, yl, scol, srow)

    def solved(a, hi_ref, lo_ref, slot):
        value = dot3(split(a), (wh[...], wl[...]), NT_DIMS)
        hi_ref[slot], lo_ref[slot] = split(value)
        return value

    def needed(slot, least):
        t = tiles[slot]
        return (t >= least) & (t <= i)

    aug[:, :size] = kernel_at(0, 0, 0, 0, True)
    factor(aug, u_ref, wh, wl, wk)
    row = lax.broadcasted_iota(jnp.int32, (size, size), 0)
    col = lax.broadcasted_iota(jnp.int32, (size, size), 1)

    @pl.when((i == 0) & (c == 0))
    def _():
        out_ref[0] = jnp.where(row <= col, u_ref[...], 0.0).T

    first = solved(kernel_at(1, 0, 1, 0), p0h, p0l, 1)

    @pl.when((i == 1) & (c == 0))
    def _():
        out_ref[0] = first

    aug[:, :size] = kernel_at(1, 1, 1, 1, True) - dot3(
        (p0h[1], p0l[1]), (p0h[1], p0l[1]), NT_DIMS
    )
    for slot in range(2, len(tiles)):

        @pl.when(needed(slot, 2))
        def _():
            value = solved(kernel_at(slot, 0, tiles[slot], 0), p0h, p0l, slot)
            if slot == 2:

                @pl.when(c == 0)
                def _():
                    out_ref[0] = value

    factor(aug, u_ref, wh, wl, wk)

    @pl.when((i == 1) & (c == 1))
    def _():
        out_ref[0] = jnp.where(row <= col, u_ref[...], 0.0).T

    for slot in range(2, len(tiles)):

        @pl.when(needed(slot, 2))
        def _():
            base = kernel_at(slot, 1, tiles[slot], 1) - dot3(
                (p0h[slot], p0l[slot]), (p0h[1], p0l[1]), NT_DIMS
            )
            value = solved(base, p1h, p1l, slot)
            if slot == 2:

                @pl.when(c == 1)
                def _():
                    out_ref[0] = value

    for k in range(blocks):
        slot = 3 + k
        t = tiles[slot]

        @pl.when(needed(slot, 2))
        def _():
            value = kernel_at(2, slot, i, t, True)
            value = value - dot3((p0h[2], p0l[2]), (p0h[slot], p0l[slot]), NT_DIMS)
            out_ref[k] = value - dot3((p1h[2], p1l[2]), (p1h[slot], p1l[slot]), NT_DIMS)

        @pl.when(t > i)
        def _():
            out_ref[k] = jnp.zeros((size, size), F32)


def plain_kernel(n_col, blocks, where_ref, band_ref, g_ref, root_ref, out_ref, *scratch):
    compute(where_ref[0], where_ref[1], n_col, blocks, g_ref, root_ref, band_ref, out_ref, *scratch)


def scratch_list(size, cov, blocks):
    slots = 3 + blocks
    return [
        pltpu.VMEM((size, 2 * size), F32),
        pltpu.VMEM((size, size), F32),
        pltpu.VMEM((size, size), BF16),
        pltpu.VMEM((size, size), BF16),
        pltpu.VMEM((NB, NB), F32),
        pltpu.VMEM((slots, size, size), BF16),
        pltpu.VMEM((slots, size, size), BF16),
        pltpu.VMEM((slots, size, size), BF16),
        pltpu.VMEM((slots, size, size), BF16),
        pltpu.VMEM((slots, size, cov), BF16),
        pltpu.VMEM((slots, size, cov), BF16),
        pltpu.VMEM((slots, size, 1), F32),
        pltpu.VMEM((slots, 8, size), F32),
    ]


def run_plain(where, band, gathered, root, n_col, blocks, interpret=False):
    size, cov = gathered.shape[1] - 8, gathered.shape[2]
    smem = pl.BlockSpec(memory_space=pltpu.SMEM)
    vmem = pl.BlockSpec(memory_space=pltpu.VMEM)
    return pl.pallas_call(
        functools.partial(plain_kernel, n_col, blocks),
        out_shape=jax.ShapeDtypeStruct((blocks, size, size), F32),
        in_specs=[smem, smem, vmem, vmem],
        out_specs=vmem,
        scratch_shapes=scratch_list(size, cov, blocks),
        compiler_params=pltpu.CompilerParams(vmem_limit_bytes=58 * 1024 * 1024),
        interpret=interpret,
    )(where, band, gathered, root)


def body(points, nugget, weights, band_start):
    n_row = lax.axis_size("row")
    n_col = lax.axis_size("col")
    blocks = n_row // n_col
    size, cov = points.shape
    where = jnp.stack([lax.axis_index("row"), lax.axis_index("col")]).astype(jnp.int32)
    extra = nugget.reshape(size // cov, cov)
    packed = jnp.concatenate([points, extra, jnp.zeros((8 - size // cov, cov), F32)])
    gathered = lax.all_gather(packed, "row")
    tiles = run_plain(where, band_start, gathered, jnp.sqrt(weights)[None, :], n_col, blocks)
    return tiles.reshape(1, blocks, 1, size, size)


def solution(mesh):
    placed = (P("row", None), P("row"), P(), P())
    return jax.shard_map(
        body,
        mesh=mesh,
        in_specs=placed,
        out_specs=P("row", None, "col", None, None),
        check_vma=False,
    )
```

```python
import functools

import jax
import jax.numpy as jnp
from jax import lax
from jax.experimental import pallas as pl
from jax.experimental.pallas import tpu as pltpu
from jax.sharding import PartitionSpec as P

F32 = jnp.float32
BF16 = jnp.bfloat16
NB = 128
GROUP = 4
NT_DIMS = (((1,), (1,)), ((), ()))
TN_DIMS = (((0,), (0,)), ((), ()))
NN_DIMS = (((1,), (0,)), ((), ()))


def split(x):
    hi = x.astype(BF16)
    return hi, (x - hi.astype(F32)).astype(BF16)


def dot3(a, b, dims):
    def one(x, y):
        return lax.dot_general(x, y, dims, preferred_element_type=F32)

    return one(a[0], b[0]) + (one(a[0], b[1]) + one(a[1], b[0]))


def wide(x):
    return jnp.broadcast_to(x, (8, NB))


def invert_factor(aug, w_ref, k):
    n_slab = NB // 8
    at = pl.multiple_of(k * NB, NB)
    block = aug[pl.ds(at, NB), pl.ds(at, NB)]
    lane = lax.broadcasted_iota(jnp.int32, (8, NB), 1)
    sub = lax.broadcasted_iota(jnp.int32, (8, NB), 0)
    s = [block[8 * t : 8 * t + 8, :] for t in range(n_slab)]
    v = [jnp.where(lane == sub + 8 * t, 1.0, 0.0).astype(F32) for t in range(n_slab)]
    for j in range(0, NB, GROUP):
        first = j // 8
        rows = [wide(s[first][j % 8 + g : j % 8 + g + 1, :]) for g in range(GROUP)]
        vrows = [wide(v[first][j % 8 + g : j % 8 + g + 1, :]) for g in range(GROUP)]
        last = (j + GROUP) // 8
        cols = [
            {t: wide(s[t][:, j + g : j + g + 1]) for t in range(last, n_slab)}
            for g in range(GROUP)
        ]
        piv = [
            {h: wide(rows[g][:, j + h : j + h + 1]) for h in range(g, GROUP)}
            for g in range(GROUP)
        ]
        for g in range(GROUP):
            root = lax.rsqrt(piv[g][g])
            inv = root * root
            w_ref[j + g : j + g + 1, :] = (vrows[g] * root)[0:1, :]
            for h in range(g + 1, GROUP):
                f = piv[g][h] * inv
                for m in range(h, GROUP):
                    piv[h][m] = piv[h][m] - f * piv[g][m]
                rows[h] = rows[h] - f * rows[g]
                vrows[h] = vrows[h] - f * vrows[g]
                for t in cols[h]:
                    cols[h][t] = cols[h][t] - f * cols[g][t]
            q = rows[g] * inv
            vq = vrows[g] * inv
            for t in cols[g]:
                s[t] = s[t] - cols[g][t] * q
                v[t] = v[t] - cols[g][t] * vq


def factor(aug, u_ref, wh, wl, wk):
    size = aug.shape[0]
    n_block = size // NB
    row = lax.broadcasted_iota(jnp.int32, (size, size), 0)
    col = lax.broadcasted_iota(jnp.int32, (size, size), 1)
    aug[:, size:] = jnp.where(row == col, 1.0, 0.0).astype(F32)

    @pl.loop(0, n_block)
    def _(k):
        invert_factor(aug, wk, k)
        winv = split(wk[...])
        for kk in range(n_block):

            @pl.when(k == kk)
            def _():
                lo, hi = kk * NB, size + (kk + 1) * NB
                strip = dot3(winv, split(aug[lo : lo + NB, lo:hi]), NN_DIMS)
                parts = split(strip)
                u_ref[lo : lo + NB, lo:] = strip[:, : size - lo]
                wh[lo : lo + NB, : lo + NB] = parts[0][:, size - lo :]
                wl[lo : lo + NB, : lo + NB] = parts[1][:, size - lo :]
                if lo + NB < size:
                    zero = jnp.zeros((NB, size - lo - NB), BF16)
                    wh[lo : lo + NB, lo + NB :] = zero
                    wl[lo : lo + NB, lo + NB :] = zero
                    left = tuple(x[:, NB : size - lo] for x in parts)
                    right = tuple(x[:, NB:] for x in parts)
                    aug[lo + NB :, lo + NB : hi] -= dot3(left, right, TN_DIMS)


def prepare(y, slot, yh, yl, scol, srow):
    hi, lo = split(y)
    yh[slot], yl[slot] = hi, lo
    sq = y * y
    scol[slot] = jnp.sum(sq, axis=1, keepdims=True)
    srow[slot] = lax.dot_general(
        jnp.ones((8, y.shape[1]), F32), sq, NT_DIMS,
        precision=lax.Precision.HIGHEST, preferred_element_type=F32,
    )


def compute(i, c, n_col, blocks, g_ref, root_ref, band_ref, out_ref,
            aug, u_ref, wh, wl, wk, p0h, p0l, p1h, p1l, yh, yl, scol, srow):
    size = aug.shape[0]
    cov = g_ref.shape[-1]
    tiles = [0, 1, i] + [c + n_col * k for k in range(blocks)]

    def kernel_at(a, b, ta, tb, nugget=False):
        cross = dot3((yh[a], yl[a]), (yh[b], yl[b]), NT_DIMS)
        dist_sq = jnp.maximum(scol[a] + srow[b][0:1, :] - 2.0 * cross, 0.0)
        dist = jnp.sqrt(3.0 * dist_sq)
        value = (1.0 + dist) * jnp.exp(-dist)
        keep = (tb >= band_ref[ta]) & (tb <= ta)
        value = jnp.where(keep, value, 0.0)
        if nugget:
            extra = jnp.concatenate(
                [g_ref[ta, size + r : size + r + 1, :] for r in range(size // cov)], axis=1
            )
            row = lax.broadcasted_iota(jnp.int32, (size, size), 0)
            col = lax.broadcasted_iota(jnp.int32, (size, size), 1)
            value = value + jnp.where((row == col) & (ta == tb), extra, 0.0)
        return value

    for slot, t in enumerate(tiles):
        y = g_ref[t, :size, :] * root_ref[...]
        prepare(y, slot, yh, yl, scol, srow)

    def solved(a, hi_ref, lo_ref, slot):
        value = dot3(split(a), (wh[...], wl[...]), NT_DIMS)
        hi_ref[slot], lo_ref[slot] = split(value)
        return value

    def needed(slot, least):
        t = tiles[slot]
        return (t >= least) & (t <= i)

    aug[:, :size] = kernel_at(0, 0, 0, 0, True)
    factor(aug, u_ref, wh, wl, wk)
    row = lax.broadcasted_iota(jnp.int32, (size, size), 0)
    col = lax.broadcasted_iota(jnp.int32, (size, size), 1)

    @pl.when((i == 0) & (c == 0))
    def _():
        out_ref[0] = jnp.where(row <= col, u_ref[...], 0.0).T

    first = solved(kernel_at(1, 0, 1, 0), p0h, p0l, 1)

    @pl.when((i == 1) & (c == 0))
    def _():
        out_ref[0] = first

    aug[:, :size] = kernel_at(1, 1, 1, 1, True) - dot3(
        (p0h[1], p0l[1]), (p0h[1], p0l[1]), NT_DIMS
    )
    for slot in range(2, len(tiles)):

        @pl.when(needed(slot, 2))
        def _():
            value = solved(kernel_at(slot, 0, tiles[slot], 0), p0h, p0l, slot)
            if slot == 2:

                @pl.when(c == 0)
                def _():
                    out_ref[0] = value

    factor(aug, u_ref, wh, wl, wk)

    @pl.when((i == 1) & (c == 1))
    def _():
        out_ref[0] = jnp.where(row <= col, u_ref[...], 0.0).T

    for slot in range(2, len(tiles)):

        @pl.when(needed(slot, 2))
        def _():
            base = kernel_at(slot, 1, tiles[slot], 1) - dot3(
                (p0h[slot], p0l[slot]), (p0h[1], p0l[1]), NT_DIMS
            )
            value = solved(base, p1h, p1l, slot)
            if slot == 2:

                @pl.when(c == 1)
                def _():
                    out_ref[0] = value

    for k in range(blocks):
        slot = 3 + k
        t = tiles[slot]

        @pl.when(needed(slot, 2))
        def _():
            value = kernel_at(2, slot, i, t, True)
            value = value - dot3((p0h[2], p0l[2]), (p0h[slot], p0l[slot]), NT_DIMS)
            out_ref[k] = value - dot3((p1h[2], p1l[2]), (p1h[slot], p1l[slot]), NT_DIMS)

        @pl.when(t > i)
        def _():
            out_ref[k] = jnp.zeros((size, size), F32)


def plain_kernel(n_col, blocks, where_ref, band_ref, g_ref, root_ref, out_ref, *scratch):
    compute(where_ref[0], where_ref[1], n_col, blocks, g_ref, root_ref, band_ref, out_ref, *scratch)


def scratch_list(size, cov, blocks):
    slots = 3 + blocks
    return [
        pltpu.VMEM((size, 2 * size), F32),
        pltpu.VMEM((size, size), F32),
        pltpu.VMEM((size, size), BF16),
        pltpu.VMEM((size, size), BF16),
        pltpu.VMEM((NB, NB), F32),
        pltpu.VMEM((slots, size, size), BF16),
        pltpu.VMEM((slots, size, size), BF16),
        pltpu.VMEM((slots, size, size), BF16),
        pltpu.VMEM((slots, size, size), BF16),
        pltpu.VMEM((slots, size, cov), BF16),
        pltpu.VMEM((slots, size, cov), BF16),
        pltpu.VMEM((slots, size, 1), F32),
        pltpu.VMEM((slots, 8, size), F32),
    ]


def run_plain(where, band, gathered, root, n_col, blocks, interpret=False):
    size, cov = gathered.shape[1] - 8 * n_col, gathered.shape[2]
    smem = pl.BlockSpec(memory_space=pltpu.SMEM)
    vmem = pl.BlockSpec(memory_space=pltpu.VMEM)
    return pl.pallas_call(
        functools.partial(plain_kernel, n_col, blocks),
        out_shape=jax.ShapeDtypeStruct((blocks, size, size), F32),
        in_specs=[smem, smem, vmem, vmem],
        out_specs=vmem,
        scratch_shapes=scratch_list(size, cov, blocks),
        compiler_params=pltpu.CompilerParams(vmem_limit_bytes=58 * 1024 * 1024),
        interpret=interpret,
    )(where, band, gathered, root)


def body(points, nugget, weights, band_start):
    n_row = lax.axis_size("row")
    n_col = lax.axis_size("col")
    blocks = n_row // n_col
    size, cov = points.shape
    where = jnp.stack([lax.axis_index("row"), lax.axis_index("col")]).astype(jnp.int32)
    extra = nugget.reshape(size // cov, cov)
    pad = 8 * n_col
    packed = jnp.concatenate([points, extra, jnp.zeros((pad - size // cov, cov), F32)])
    share = (size + pad) // n_col
    mine = lax.dynamic_slice_in_dim(packed, lax.axis_index("col") * share, share)
    gathered = lax.all_gather(mine, ("row", "col"), tiled=True)
    gathered = gathered.reshape(n_row, size + pad, cov)
    tiles = run_plain(where, band_start, gathered, jnp.sqrt(weights)[None, :], n_col, blocks)
    return tiles.reshape(1, blocks, 1, size, size)


def solution(mesh):
    placed = (P("row", None), P("row"), P(), P())
    return jax.shard_map(
        body,
        mesh=mesh,
        in_specs=placed,
        out_specs=P("row", None, "col", None, None),
        check_vma=False,
    )
```
